512 devices in a mesh: pipe: 4 (over z_lo, core), expert: 32 (over y, z_hi), tensor: 4 (over x).
Axes of the slice: x: 4, y: 8, z: 8 (z_hi: 4, z_lo: 2; z = z_hi * 2 + z_lo), core: 2. Of those that a mesh axis runs over, the one named last changes fastest.
Arguments:
- context: bfloat16 [4, 8192, 2048], P('pipe', 'expert', 'tensor'), may hold values from -6 to 6
- attn_weight: bfloat16 [4, 2048, 2048], P('pipe', 'tensor', 'expert'), may hold values from -0.125 to 0.125
- residual: bfloat16 [4, 8192, 2048], P('pipe', ('expert', 'tensor')), may hold values from -6 to 6
- norm_gain: float32 [4, 2048], P('pipe'), may hold values from 0.25 to 1.75
- centroid: bfloat16 [4, 4, 2048], P('pipe', 'tensor'), may hold values from -0.25 to 0.25
- w_in: bfloat16 [4, 4, 2048, 8192], P('pipe', 'tensor', None, 'expert'), may hold values from -0.125 to 0.125
- w_out: bfloat16 [4, 4, 8192, 2048], P('pipe', 'tensor', 'expert'), may hold values from -0.0625 to 0.0625
- route_order: int32 [4, 128, 64], P('pipe', ('expert', 'tensor')), may hold values from 0 to 63, each once within a row
Outputs:
- handed: bfloat16 [4, 8192, 2048], P('pipe', ('expert', 'tensor'))
The draws below stay inside these ranges and needn't reach their ends.
Inputs may be any that keep to these rules, and one draw needn't show every extreme that they name: `route_order`: each row of 64 numbers is a permutation of 0 to 63.
All inputs are finite; a program needn't handle non-finite values.
Results may differ from the reference program's by a relative error of at most 0.018.
Values may be sent and summed in bfloat16 or wider, within the bound.
A program may use at most 64 MiB of HBM per device.

```python
import jax
import jax.numpy as jnp
from jax import lax

D = 2048
FF = 8192
ROWS = 64
TOKENS = 8192
EXPERTS = 4
N_PIPE = 4
N_EXPERT = 32
N_TENSOR = 4


def block_levels(own_key, extent, cuts, smallest, high):
    loudness, own = 1.0, jax.random.fold_in(own_key, 6)
    for position, blocks in cuts:
        draws = jnp.exp(jax.random.uniform(jax.random.fold_in(own, position), (blocks,), jnp.float32, smallest / len(cuts), high / len(cuts)))
        loudness = loudness * jnp.repeat(draws, extent[position] // blocks).reshape([-1 if axis == position else 1 for axis in range(len(extent))])
    return loudness


def noise(rng, dims, scale, limit, split=(), dtype=jnp.bfloat16):
    result = jax.random.normal(rng, dims, jnp.float32) * scale
    if len(split) > 0:
        result = block_levels(rng, dims, split, -0.22, 0.18) * result
    return jnp.clip(result, min=-limit, max=limit).astype(dtype)


def setup_inputs(seed: int = 0) -> dict:
    splits = jax.random.split(jax.random.key(seed), 9)
    context = noise(splits[0], (N_PIPE, TOKENS, D), 1.0, 6.0, ((0, 4), (1, 32), (2, 4)))
    attn_weight = noise(splits[1], (N_PIPE, D, D), D ** -0.5, 0.125, ((0, 4), (1, 4), (2, 32)))
    residual = noise(splits[2], (N_PIPE, TOKENS, D), 1.0, 6.0, ((0, 4), (1, 128)))
    norm_gain = jnp.clip(1.0 + 0.15 * jax.random.normal(splits[3], (N_PIPE, D), jnp.float32), 0.25, 1.75)
    centroid = noise(splits[4], (N_PIPE, EXPERTS, D), (D / 4) ** -0.5, 0.25, ((0, 4), (1, 4)))
    w_in = noise(splits[5], (N_PIPE, EXPERTS, D, FF), D ** -0.5, 0.125, ((0, 4), (1, 4), (3, 32)))
    w_out = noise(splits[6], (N_PIPE, EXPERTS, FF, D), FF ** -0.5, 0.0625, ((0, 4), (1, 4), (2, 32)))
    route_order = jax.vmap(lambda own: jax.random.permutation(own, ROWS))(jax.random.split(splits[7], N_PIPE * (N_EXPERT * N_TENSOR))).reshape((N_PIPE, N_EXPERT * N_TENSOR, ROWS)).astype(jnp.int32)
    return dict(context=context, attn_weight=attn_weight, residual=residual, norm_gain=norm_gain, centroid=centroid, w_in=w_in, w_out=w_out, route_order=route_order)


def expert_reply(rows_in, first, second, gating):
    up_values = jnp.dot(rows_in, first, preferred_element_type=jnp.float32)
    activated = jax.nn.gelu(up_values, approximate=True).astype(jnp.bfloat16)
    group_width = FF // N_EXPERT
    act_groups = jnp.transpose(activated.reshape(rows_in.shape[0], N_EXPERT, group_width), (1, 0, 2))
    out_groups = second.reshape(N_EXPERT, group_width, D)

    def accumulate(total, operands):
        act_piece, weight_piece = operands
        term = jnp.dot(act_piece, weight_piece, preferred_element_type=jnp.float32).astype(jnp.bfloat16)
        return (total + term.astype(jnp.float32), None)
    summed, unused = lax.scan(accumulate, jnp.zeros((rows_in.shape[0], D), jnp.float32), (act_groups, out_groups))
    affinity = jnp.dot(rows_in, gating, preferred_element_type=jnp.float32)
    return (jax.nn.sigmoid(affinity)[:, None] * summed).astype(jnp.bfloat16)

def reference(context, attn_weight, residual, norm_gain, centroid, w_in, w_out, route_order):
    per_peer = ROWS // N_TENSOR
    results = []
    for section in range(N_PIPE):
        attended = jnp.dot(context[section], attn_weight[section], preferred_element_type=jnp.float32)
        hidden = (residual[section].astype(jnp.float32) + attended).astype(jnp.bfloat16)
        hidden_f = hidden.astype(jnp.float32)
        inverse_rms = lax.rsqrt(lax.optimization_barrier(jnp.mean(hidden_f * hidden_f, axis=-1, keepdims=True)) + 1e-05)
        normed = (hidden_f * inverse_rms * norm_gain[section][None, :]).astype(jnp.bfloat16)
        blocks = normed.reshape(N_EXPERT * N_TENSOR, ROWS, D)
        order_rows = route_order[section]
        outgoing = jnp.take_along_axis(blocks, order_rows[:, :, None], axis=1)
        split_out = outgoing.reshape(N_EXPERT, N_TENSOR, N_TENSOR, per_peer, D)
        arrived = jnp.transpose(split_out, (0, 2, 1, 3, 4)).reshape(N_EXPERT, N_TENSOR, ROWS, D)
        replies = []
        for expert_id in range(N_TENSOR):
            rows_in = arrived[:, expert_id].reshape(N_EXPERT * ROWS, D)
            answer = expert_reply(rows_in, w_in[section, expert_id], w_out[section, expert_id], centroid[section, expert_id])
            replies.append(answer.reshape(N_EXPERT, ROWS, D))
        reply = jnp.stack(replies, axis=1)
        split_back = reply.reshape(N_EXPERT, N_TENSOR, N_TENSOR, per_peer, D)
        returned = jnp.transpose(split_back, (0, 2, 1, 3, 4)).reshape(N_EXPERT * N_TENSOR, ROWS, D)
        inverse = jnp.argsort(order_rows, axis=-1).astype(jnp.int32)
        expert_out = jnp.take_along_axis(returned, inverse[:, :, None], axis=1)
        layer_out = (hidden_f + expert_out.reshape(TOKENS, D).astype(jnp.float32)).astype(jnp.bfloat16)
        results.append(layer_out)
    stacked = jnp.stack(results)
    return jnp.roll(stacked, 1, axis=0)
```

```python
import math

import jax
import jax.numpy as jnp
from jax import lax
from jax.experimental import pallas as pl
from jax.experimental.pallas import tpu as pltpu
from jax.sharding import PartitionSpec as P

MESH = pl.DeviceIdType.MESH
F32, BF16 = jnp.float32, jnp.bfloat16
NY, NZ, NX, NP = 8, 4, 4, 4
D, ROWS, HEADS, UNITS = 2048, 64, 512, 256
OFFSETS = (0, 1, -1, 2, -2, 3, -3, 4)
SLOT = {0: 0, 1: 1, -1: 2, 2: 3, -2: 4, 3: 5, -3: 6, 4: 7, -4: 7}
HOPS = 4
DIRS = ((0, 1), (1, -1))
X_BATCHES = ((0, 3), (3, 2), (5, 2), (7, 1))
AG_ORDER = ((0, 1), (2, 3))


def gelu(u):
    inner = math.sqrt(2.0 / math.pi) * (u + 0.044715 * (u * u * u))
    return 0.5 * u * (1.0 + jnp.tanh(inner))


def body(
    ctx, attn, res, gain, cent, w_in, w_out, order, out,
    proj, part, from_x, hidden, outgoing, tokens, w1, w2, act, sums,
    rs_out, rs_in, z_out, z_in, reply, returned, layer, affinity, onehot,
    local_sem, wz_send, wz_recv, pz_send, pz_recv, py_send, py_recv, ax_send, ax_recv,
    dx_send, dx_recv, tz_send, tz_recv, ty_send, ty_recv, ry_send, ry_recv,
    rz_send, rz_recv, bx_send, bx_recv, hp_send, hp_recv,
):
    p, e, t = lax.axis_index("pipe"), lax.axis_index("expert"), lax.axis_index("tensor")
    y, z = e // NZ, e % NZ

    def at_y(step):
        return (p, (y + step + NY) % NY * NZ + z, t)

    def at_z(step):
        return (p, y * NZ + (z + step + NZ) % NZ, t)

    def at_x(step):
        return (p, e, (t + step) % NX)

    pending = []

    def send(src, dst, s_sem, r_sem, to):
        copy = pltpu.make_async_remote_copy(
            src_ref=src, dst_ref=dst, send_sem=s_sem, recv_sem=r_sem,
            device_id=to, device_id_type=MESH,
        )
        copy.start()
        pending.append(copy)
        return copy

    barrier = pltpu.get_barrier_semaphore()
    friends = [at_y(1), at_y(-1), at_z(1), at_z(-1), at_z(2), at_x(1), at_x(2), at_x(3)]
    friends += [((p + 1) % NP, e, t), ((p + NP - 1) % NP, e, t)]
    for friend in friends:
        pl.semaphore_signal(barrier, inc=1, device_id=friend, device_id_type=MESH)

    own_w = (
        pltpu.make_async_copy(w_in, w1.at[:, pl.ds(0, UNITS)], local_sem.at[0]),
        pltpu.make_async_copy(w_out, w2.at[pl.ds(0, UNITS)], local_sem.at[1]),
    )
    for copy in own_w:
        copy.start()

    eye = (
        lax.broadcasted_iota(jnp.int32, (ROWS, ROWS), 0)
        == lax.broadcasted_iota(jnp.int32, (ROWS, ROWS), 1)
    ).astype(BF16)
    columns = lax.dot_general(eye, attn[...], (((1,), (1,)), ((), ())), preferred_element_type=F32)
    proj[0, pl.ds(pl.multiple_of(z * ROWS, ROWS), ROWS), :] = columns.astype(BF16)
    onehot[...] = (lax.broadcasted_iota(jnp.int32, (ROWS, ROWS), 0) == order[...]).astype(BF16)

    pl.semaphore_wait(barrier, len(friends))

    def proj_rows(slot, plane, start=0, count=ROWS):
        return proj.at[slot, pl.ds(pl.multiple_of(plane * ROWS + start, 32), count)]

    planes = (z, (z + NZ - 1) % NZ, (z + 1) % NZ, (z + 2) % NZ)
    pz = [
        send(proj_rows(0, z), proj_rows(0, z), pz_send.at[i], pz_recv.at[i], at_z(step))
        for i, step in enumerate((1, -1, 2))
    ]

    def ring(view, flow, hop, s_sem, r_sem):
        made = []
        for i, step in DIRS:
            part_of = None if hop < HOPS - 1 else i
            src = view(flow, SLOT[-step * hop], part_of)
            dst = view(flow, SLOT[-step * (hop + 1)], part_of)
            made.append(
                send(src, dst, s_sem.at[flow, hop, i], r_sem.at[flow, hop, i], at_y(step))
            )
        return made

    def proj_view(flow, slot, half):
        if half is None:
            return proj_rows(slot, planes[flow])
        return proj_rows(slot, planes[flow], half * 32, 32)

    flying = [ring(proj_view, 0, 0, py_send, py_recv)]

    half = UNITS // 2
    wz = []
    for i, step in DIRS:
        cols = pl.ds(i * half, half)
        there = pl.ds(UNITS + i * half, half)
        wz.append(send(w_in.at[:, cols], w1.at[:, there], wz_send.at[i], wz_recv.at[i], at_z(step)))
    for i, step in DIRS:
        cols = pl.ds(i * half, half)
        there = pl.ds(UNITS + i * half, half)
        wz.append(send(w_out.at[cols], w2.at[there], wz_send.at[2 + i], wz_recv.at[2 + i], at_z(step)))

    for flow in (1, 2, 3):
        pz[flow - 1].wait_recv()
        flying.append(ring(proj_view, flow, 0, py_send, py_recv))

    def project(slot):
        value = lax.dot_general(
            ctx[...], proj[slot], (((1,), (1,)), ((), ())), preferred_element_type=F32
        )
        part[slot] = value.astype(BF16)

    def share(batch):
        first, count = X_BATCHES[batch]
        made = []
        for step in (1, 2, 3):
            rows = pl.ds(pl.multiple_of((t + step) % NX * ROWS, ROWS), ROWS)
            made.append(
                send(
                    part.at[pl.ds(first, count), rows],
                    from_x.at[step - 1, pl.ds(first, count)],
                    ax_send.at[batch, step - 1], ax_recv.at[batch, step - 1], at_x(step),
                )
            )
        return made

    project(0)
    shared = []
    for hop in range(1, HOPS):
        for flow in range(4):
            for copy in flying[flow]:
                copy.wait_recv()
            flying[flow] = ring(proj_view, flow, hop, py_send, py_recv)
        project(2 * hop - 1)
        project(2 * hop)
        shared.append(share(hop - 1))
    for flow in range(4):
        for copy in flying[flow]:
            copy.wait_recv()
    project(7)
    shared.append(share(3))

    squares = jnp.zeros((ROWS, 1), F32)
    for batch, (first, count) in enumerate(X_BATCHES):
        for copy in shared[batch]:
            copy.wait_recv()
        for slot in range(first, first + count):
            mine = part[slot, pl.ds(pl.multiple_of(t * ROWS, ROWS), ROWS), :].astype(F32)
            attended = mine
            for other in range(3):
                attended = attended + from_x[other, slot].astype(F32)
            cols = pl.ds(pl.multiple_of((y + OFFSETS[slot] + NY) % NY * 256, 256), 256)
            value = (res[:, cols].astype(F32) + attended).astype(BF16)
            hidden[:, cols] = value
            wide = value.astype(F32)
            squares = squares + jnp.sum(wide * wide, axis=-1, keepdims=True)
    inverse_rms = lax.rsqrt(squares * (1.0 / D) + 1e-05)
    for c in range(4):
        cols = pl.ds(c * 512, 512)
        normed = (hidden[:, cols].astype(F32) * inverse_rms * gain[:, cols]).astype(BF16)
        picked = lax.dot_general(
            onehot[...], normed, (((0,), (0,)), ((), ())), preferred_element_type=F32
        )
        outgoing[:, cols] = picked.astype(BF16)

    def sixteen(k):
        return pl.ds(pl.multiple_of(k * 16, 16), 16)

    dx = []
    for step in (1, 2, 3):
        dx.append(
            send(
                outgoing.at[sixteen((t + step) % NX)], tokens.at[0, 0, sixteen(t)],
                dx_send.at[step - 1], dx_recv.at[step - 1], at_x(step),
            )
        )
    tokens[0, 0, sixteen(t), :] = outgoing[sixteen(t), :]
    for copy in dx:
        copy.wait_recv()

    def token_view(flow, slot, quarter):
        start, count = flow % 2 * 32, 32
        if quarter is not None:
            start, count = start + quarter * 16, 16
        return tokens.at[flow // 2, slot, pl.ds(start, count)]

    flying = [ring(token_view, flow, 0, ty_send, ty_recv) for flow in (0, 1)]
    tz = []
    for i in range(2):
        rows = pl.ds(i * 32, 32)
        tz.append(
            send(tokens.at[0, 0, rows], tokens.at[1, 0, rows], tz_send.at[i], tz_recv.at[i], at_z(2))
        )

    dots = jnp.zeros((ROWS, 1), F32)
    for c in range(4):
        cols = pl.ds(c * 512, 512)
        dots = dots + jnp.sum(
            tokens[0, 0, :, cols].astype(F32) * cent[:, cols].astype(F32), axis=-1, keepdims=True
        )
    affinity[...] = jnp.broadcast_to(1.0 / (1.0 + jnp.exp(-dots)), (ROWS, 128))

    def pass_on(flow, hop):
        for copy in flying[flow]:
            copy.wait_recv()
        flying[flow] = ring(token_view, flow, hop, ty_send, ty_recv)

    def expert(source, first):
        rows = pl.ds(first * ROWS, 4 * ROWS)
        block = tokens.at[source, pl.ds(first, 4)]

        def up(j, carry):
            cols = pl.ds(pl.multiple_of(j * 256, 256), 256)
            value = jnp.dot(
                block[...].reshape(4 * ROWS, D), w1[:, cols], preferred_element_type=F32
            )
            act[:, cols] = gelu(value).astype(BF16)
            return carry

        lax.fori_loop(0, 2, up, 0)

        def down(j, carry):
            cols = pl.ds(pl.multiple_of(j * 512, 512), 512)
            sums[source, rows, cols] = jnp.dot(act[...], w2[:, cols], preferred_element_type=F32)
            return carry

        lax.fori_loop(0, 4, down, 0)

    for hop in range(1, HOPS):
        for flow in (0, 1):
            pass_on(flow, hop)
    for i in range(2):
        tz[i].wait_recv()
        flying.append(ring(token_view, 2 + i, 0, ty_send, ty_recv))
    for copy in own_w:
        copy.wait()
    for copy in wz:
        copy.wait_recv()
    expert(0, 0)
    for flow in (2, 3):
        pass_on(flow, 1)
    for flow in (0, 1):
        for copy in flying[flow]:
            copy.wait_recv()
    expert(0, 4)
    for flow in (2, 3):
        pass_on(flow, 2)

    rs = {}

    def back(flow, hop):
        source, base = flow // 2, flow % 2 * 32
        for i, step in DIRS:
            slot = SLOT[step * (HOPS - hop)]
            start = slot * ROWS + base
            if hop == 0:
                count = 16
                rs_out[flow, hop, i, pl.ds(0, 16), :] = sums[
                    source, pl.ds(start + i * 16, 16), :
                ].astype(BF16)
            else:
                count = 32
                rs[flow, hop - 1][i].wait_recv()
                for quarter in range(2):
                    rows = pl.ds(quarter * 16, 16)
                    value = sums[source, pl.ds(start + quarter * 16, 16), :]
                    if hop > 1:
                        value = value + rs_in[flow, hop - 1, i, rows, :].astype(F32)
                    elif quarter == i:
                        value = value + rs_in[flow, 0, i, pl.ds(0, 16), :].astype(F32)
                    rs_out[flow, hop, i, rows, :] = value.astype(BF16)
            rs.setdefault((flow, hop), []).append(
                send(
                    rs_out.at[flow, hop, i, pl.ds(0, count)],
                    rs_in.at[flow, hop, i, pl.ds(0, count)],
                    ry_send.at[flow, hop, i], ry_recv.at[flow, hop, i], at_y(step),
                )
            )

    def total(flow):
        source, base = flow // 2, flow % 2 * 32
        for copy in rs[flow, HOPS - 1]:
            copy.wait_recv()
        value = sums[source, pl.ds(base, 32), :]
        for i in range(2):
            value = value + rs_in[flow, HOPS - 1, i].astype(F32)
        return value

    back(0, 0)
    back(1, 0)
    expert(1, 0)
    for flow in (2, 3):
        pass_on(flow, 3)
    back(0, 1)
    back(1, 1)
    for flow in (2, 3):
        for copy in flying[flow]:
            copy.wait_recv()
    expert(1, 4)
    rz = []
    for flow, hop in ((2, 0), (3, 0), (0, 2), (2, 1), (3, 1), (2, 2), (3, 2), (2, 3), (3, 3)):
        back(flow, hop)
    back(1, 2)

    def home(i):
        z_out[i] = total(2 + i).astype(BF16)
        rz.append(send(z_out.at[i], z_in.at[i], rz_send.at[i], rz_recv.at[i], at_z(2)))

    home(0)
    back(0, 3)
    home(1)
    back(1, 3)
    for i in range(2):
        value = total(i)
        rz[i].wait_recv()
        value = value + z_in[i].astype(F32)
        rows = pl.ds(i * 32, 32)
        reply[rows, :] = (affinity[rows, :1] * value).astype(BF16)

    bx = []
    for step in (1, 2, 3):
        bx.append(
            send(
                reply.at[sixteen((t + step) % NX)], returned.at[sixteen(t)],
                bx_send.at[step - 1], bx_recv.at[step - 1], at_x(step),
            )
        )
    returned[sixteen(t), :] = reply[sixteen(t), :]
    for copy in bx:
        copy.wait_recv()
    for c in range(4):
        cols = pl.ds(c * 512, 512)
        placed = jnp.dot(onehot[...], returned[:, cols], preferred_element_type=F32)
        layer[:, cols] = (
            hidden[:, cols].astype(F32) + placed.astype(BF16).astype(F32)
        ).astype(BF16)
    last = send(layer, out, hp_send, hp_recv, ((p + 1) % NP, e, t))
    last.wait_recv()
    for copy in pending:
        copy.wait_send()


def shards(context, attn_weight, residual, norm_gain, centroid, w_in, w_out, route_order):
    vmem, hbm = pl.BlockSpec(memory_space=pltpu.VMEM), pl.BlockSpec(memory_space=pl.ANY)
    dma = pltpu.SemaphoreType.DMA
    flows = (4, HOPS, 2)
    result = pl.pallas_call(
        body,
        out_shape=jax.ShapeDtypeStruct((ROWS, D), BF16),
        in_specs=[vmem, vmem, vmem, vmem, vmem, hbm, hbm, vmem],
        out_specs=hbm,
        scratch_shapes=[
            pltpu.VMEM((NY, 4 * ROWS, HEADS), BF16),
            pltpu.VMEM((NY, 4 * ROWS, 256), BF16),
            pltpu.VMEM((3, NY, ROWS, 256), BF16),
            pltpu.VMEM((ROWS, D), BF16),
            pltpu.VMEM((ROWS, D), BF16),
            pltpu.VMEM((2, NY, ROWS, D), BF16),
            pltpu.VMEM((D, 2 * UNITS), BF16),
            pltpu.VMEM((2 * UNITS, D), BF16),
            pltpu.VMEM((4 * ROWS, 2 * UNITS), BF16),
            pltpu.VMEM((2, NY * ROWS, D), F32),
            pltpu.VMEM((4, HOPS, 2, 32, D), BF16),
            pltpu.VMEM((4, HOPS, 2, 32, D), BF16),
            pltpu.VMEM((2, 32, D), BF16),
            pltpu.VMEM((2, 32, D), BF16),
            pltpu.VMEM((ROWS, D), BF16),
            pltpu.VMEM((ROWS, D), BF16),
            pltpu.VMEM((ROWS, D), BF16),
            pltpu.VMEM((ROWS, 128), F32),
            pltpu.VMEM((ROWS, ROWS), BF16),
            dma((2,)),
            dma((4,)), dma((4,)),
            dma((3,)), dma((3,)),
            dma(flows), dma(flows),
            dma((4, 3)), dma((4, 3)),
            dma((3,)), dma((3,)),
            dma((2,)), dma((2,)),
            dma(flows), dma(flows),
            dma(flows), dma(flows),
            dma((2,)), dma((2,)),
            dma((3,)), dma((3,)),
            dma, dma,
        ],
        compiler_params=pltpu.CompilerParams(
            collective_id=0, has_side_effects=True, vmem_limit_bytes=48 * 2**20
        ),
        cost_estimate=pl.CostEstimate(
            flops=4_800_000_000, bytes_accessed=4_000_000, transcendentals=600_000
        ),
    )(
        context[0], attn_weight[0], residual[0], norm_gain, centroid[0],
        w_in[0, 0], w_out[0, 0], route_order[0],
    )
    return result[None]


def solution(mesh):
    return jax.shard_map(
        shards,
        mesh=mesh,
        in_specs=(
            P("pipe", "expert", "tensor"),
            P("pipe", "tensor", "expert"),
            P("pipe", ("expert", "tensor"), None),
            P("pipe", None),
            P("pipe", "tensor", None),
            P("pipe", "tensor", None, "expert"),
            P("pipe", "tensor", "expert", None),
            P("pipe", ("expert", "tensor"), None),
        ),
        out_specs=P("pipe", ("expert", "tensor"), None),
        check_vma=False,
    )
```

```python
import math

import jax
import jax.numpy as jnp
from jax import lax
from jax.experimental import pallas as pl
from jax.experimental.pallas import tpu as pltpu
from jax.sharding import PartitionSpec as P

MESH = pl.DeviceIdType.MESH
F32, BF16 = jnp.float32, jnp.bfloat16
NY, NZ, NX, NP = 8, 4, 4, 4
D, ROWS, HEADS, UNITS = 2048, 64, 512, 256
WIDE = D // 2
OFFSETS = (0, 1, -1, 2, -2, 3, -3, 4)
SLOT = {0: 0, 1: 1, -1: 2, 2: 3, -2: 4, 3: 5, -3: 6, 4: 7, -4: 7}
HOPS = 4
DIRS = ((0, 1), (1, -1))
X_BATCHES = ((0, 3), (3, 2), (5, 2), (7, 1))


def gelu(u):
    inner = math.sqrt(2.0 / math.pi) * (u + 0.044715 * (u * u * u))
    return 0.5 * u * (1.0 + jnp.tanh(inner))


def body(
    ctx_hbm, attn_hbm, res_hbm, gain_hbm, cent_hbm, w_in, w_out, order_hbm, out,
    ctx, res, gain, cent, order, proj, part, from_x, hidden, outgoing, tokens, w1, w2, act, sums,
    rs_out, rs_in, z_out, z_in, reply, returned, layer, affinity, onehot,
    local_sem, wz_send, wz_recv, pz_send, pz_recv, py_send, py_recv, ax_send, ax_recv,
    dx_send, dx_recv, tz_send, tz_recv, ty_send, ty_recv, ry_send, ry_recv,
    rz_send, rz_recv, bx_send, bx_recv, hp_send, hp_recv,
):
    p, e, t = lax.axis_index("pipe"), lax.axis_index("expert"), lax.axis_index("tensor")
    y, z = e // NZ, e % NZ

    def at_y(step):
        return (p, (y + step + NY) % NY * NZ + z, t)

    def at_z(step):
        return (p, y * NZ + (z + step + NZ) % NZ, t)

    def at_x(step):
        return (p, e, (t + step) % NX)

    pending = []

    def send(src, dst, s_sem, r_sem, to):
        copy = pltpu.make_async_remote_copy(
            src_ref=src, dst_ref=dst, send_sem=s_sem, recv_sem=r_sem,
            device_id=to, device_id_type=MESH,
        )
        copy.start()
        pending.append(copy)
        return copy

    barrier = pltpu.get_barrier_semaphore()
    friends = [at_y(1), at_y(-1), at_z(1), at_z(-1), at_z(2), at_x(1), at_x(2), at_x(3)]
    friends += [((p + 1) % NP, e, t), ((p + NP - 1) % NP, e, t)]
    for friend in friends:
        pl.semaphore_signal(barrier, inc=1, device_id=friend, device_id_type=MESH)

    def proj_rows(slot, plane, start=0, count=ROWS):
        return proj.at[slot, pl.ds(pl.multiple_of(plane * ROWS + start, 32), count)]

    loads = [
        pltpu.make_async_copy(src, dst, local_sem.at[i])
        for i, (src, dst) in enumerate((
            (attn_hbm, proj_rows(0, z)), (ctx_hbm, ctx), (res_hbm, res), (gain_hbm, gain),
            (cent_hbm, cent), (order_hbm, order),
            (w_in, w1.at[:, pl.ds(0, UNITS)]), (w_out, w2.at[pl.ds(0, UNITS)]),
        ))
    ]
    for copy in loads:
        copy.start()
    loads[0].wait()
    pl.semaphore_wait(barrier, len(friends))

    planes = (z, (z + NZ - 1) % NZ, (z + 1) % NZ, (z + 2) % NZ)
    pz = [
        send(proj_rows(0, z), proj_rows(0, z), pz_send.at[i], pz_recv.at[i], at_z(step))
        for i, step in enumerate((1, -1, 2))
    ]

    def ring(view, flow, hop, s_sem, r_sem):
        made = []
        for i, step in DIRS:
            part_of = None if hop < HOPS - 1 else i
            src = view(flow, SLOT[-step * hop], part_of)
            dst = view(flow, SLOT[-step * (hop + 1)], part_of)
            made.append(
                send(src, dst, s_sem.at[flow, hop, i], r_sem.at[flow, hop, i], at_y(step))
            )
        return made

    def proj_view(flow, slot, half):
        if half is None:
            return proj_rows(slot, planes[flow])
        return proj_rows(slot, planes[flow], half * 32, 32)

    flying = [ring(proj_view, 0, 0, py_send, py_recv)]

    for flow in (1, 2, 3):
        pz[flow - 1].wait_recv()
        flying.append(ring(proj_view, flow, 0, py_send, py_recv))

    half = UNITS // 2

    def units(i):
        return pl.ds(i * half, half), pl.ds(UNITS + i * half, half)

    wz_in = []
    for i, step in DIRS:
        mine, there = units(i)
        wz_in.append(
            send(w_in.at[:, mine], w1.at[:, there], wz_send.at[i], wz_recv.at[i], at_z(step))
        )

    def project(slot):
        value = lax.dot_general(
            ctx[...], proj[slot], (((1,), (1,)), ((), ())), preferred_element_type=F32
        )
        part[slot] = value.astype(BF16)

    def share(batch):
        first, count = X_BATCHES[batch]
        made = []
        for step in (1, 2, 3):
            rows = pl.ds(pl.multiple_of((t + step) % NX * ROWS, ROWS), ROWS)
            made.append(
                send(
                    part.at[pl.ds(first, count), rows],
                    from_x.at[step - 1, pl.ds(first, count)],
                    ax_send.at[batch, step - 1], ax_recv.at[batch, step - 1], at_x(step),
                )
            )
        return made

    loads[1].wait()
    project(0)
    for copy in loads[2:6]:
        copy.wait()
    onehot[...] = (lax.broadcasted_iota(jnp.int32, (ROWS, ROWS), 0) == order[...]).astype(BF16)
    shared = []
    for hop in range(1, HOPS):
        for flow in range(4):
            for copy in flying[flow]:
                copy.wait_recv()
            flying[flow] = ring(proj_view, flow, hop, py_send, py_recv)
        project(2 * hop - 1)
        project(2 * hop)
        shared.append(share(hop - 1))
    for flow in range(4):
        for copy in flying[flow]:
            copy.wait_recv()
    project(7)
    shared.append(share(3))

    squares = jnp.zeros((ROWS, 1), F32)
    for batch, (first, count) in enumerate(X_BATCHES):
        for copy in shared[batch]:
            copy.wait_recv()
        for slot in range(first, first + count):
            mine = part[slot, pl.ds(pl.multiple_of(t * ROWS, ROWS), ROWS), :].astype(F32)
            attended = mine
            for other in range(3):
                attended = attended + from_x[other, slot].astype(F32)
            cols = pl.ds(pl.multiple_of((y + OFFSETS[slot] + NY) % NY * 256, 256), 256)
            value = (res[:, cols].astype(F32) + attended).astype(BF16)
            hidden[:, cols] = value
            wide = value.astype(F32)
            squares = squares + jnp.sum(wide * wide, axis=-1, keepdims=True)
    inverse_rms = lax.rsqrt(squares * (1.0 / D) + 1e-05)
    for c in range(4):
        cols = pl.ds(c * 512, 512)
        normed = (hidden[:, cols].astype(F32) * inverse_rms * gain[:, cols]).astype(BF16)
        picked = lax.dot_general(
            onehot[...], normed, (((0,), (0,)), ((), ())), preferred_element_type=F32
        )
        outgoing[:, cols] = picked.astype(BF16)

    def sixteen(k):
        return pl.ds(pl.multiple_of(k * 16, 16), 16)

    dx = []
    for step in (1, 2, 3):
        dx.append(
            send(
                outgoing.at[sixteen((t + step) % NX)], tokens.at[0, 0, sixteen(t)],
                dx_send.at[step - 1], dx_recv.at[step - 1], at_x(step),
            )
        )
    tokens[0, 0, sixteen(t), :] = outgoing[sixteen(t), :]
    for copy in dx:
        copy.wait_recv()

    def token_view(flow, slot, quarter):
        start, count = flow % 2 * 32, 32
        if quarter is not None:
            start, count = start + quarter * 16, 16
        return tokens.at[flow // 2, slot, pl.ds(start, count)]

    flying = [ring(token_view, flow, 0, ty_send, ty_recv) for flow in (0, 1)]
    tz = []
    for i in range(2):
        rows = pl.ds(i * 32, 32)
        tz.append(
            send(tokens.at[0, 0, rows], tokens.at[1, 0, rows], tz_send.at[i], tz_recv.at[i], at_z(2))
        )

    dots = jnp.zeros((ROWS, 1), F32)
    for c in range(4):
        cols = pl.ds(c * 512, 512)
        dots = dots + jnp.sum(
            tokens[0, 0, :, cols].astype(F32) * cent[:, cols].astype(F32), axis=-1, keepdims=True
        )
    affinity[...] = jnp.broadcast_to(1.0 / (1.0 + jnp.exp(-dots)), (ROWS, 128))

    def pass_on(flow, hop):
        for copy in flying[flow]:
            copy.wait_recv()
        flying[flow] = ring(token_view, flow, hop, ty_send, ty_recv)

    def up(source, first):
        def tile(j, carry):
            cols = pl.ds(pl.multiple_of(j * 256, 256), 256)
            value = jnp.dot(
                tokens[source, pl.ds(first, 4)].reshape(4 * ROWS, D), w1[:, cols],
                preferred_element_type=F32,
            )
            act[source, pl.ds(first * ROWS, 4 * ROWS), cols] = gelu(value).astype(BF16)
            return carry

        lax.fori_loop(0, 2, tile, 0)

    def down(source, first):
        rows = pl.ds(first * ROWS, 4 * ROWS)

        def tile(j, carry):
            cols = pl.ds(pl.multiple_of(j * 512, 512), 512)
            sums[source, rows, cols] = jnp.dot(
                act[source, rows, :], w2[:, cols], preferred_element_type=F32
            )
            return carry

        lax.fori_loop(0, 4, tile, 0)

    for hop in range(1, HOPS):
        for flow in (0, 1):
            pass_on(flow, hop)
    for i in range(2):
        tz[i].wait_recv()
        flying.append(ring(token_view, 2 + i, 0, ty_send, ty_recv))
    wz_out = []
    for i, step in DIRS:
        mine, there = units(i)
        wz_out.append(
            send(w_out.at[mine], w2.at[there], wz_send.at[2 + i], wz_recv.at[2 + i], at_z(step))
        )
    for copy in loads[6:]:
        copy.wait()
    for copy in wz_in:
        copy.wait_recv()
    up(0, 0)
    for flow in (2, 3):
        pass_on(flow, 1)
    for flow in (0, 1):
        for copy in flying[flow]:
            copy.wait_recv()
    up(0, 4)
    for flow in (2, 3):
        pass_on(flow, 2)
    up(1, 0)
    for flow in (2, 3):
        pass_on(flow, 3)
    for copy in wz_out:
        copy.wait_recv()
    down(0, 4)

    rs = {}

    def back(flow, hop):
        source, cols = flow // 2, pl.ds(flow % 2 * WIDE, WIDE)
        for i, step in DIRS:
            start = SLOT[step * (HOPS - hop)] * ROWS
            count = 32 if hop == 0 else ROWS
            if hop == 0:
                rs_out[flow, hop, i, pl.ds(0, 32), :] = sums[
                    source, pl.ds(start + i * 32, 32), cols
                ].astype(BF16)
            else:
                rs[flow, hop - 1][i].wait_recv()
                for part_of in range(2):
                    rows = pl.ds(part_of * 32, 32)
                    value = sums[source, pl.ds(start + part_of * 32, 32), cols]
                    if hop > 1:
                        value = value + rs_in[flow, hop - 1, i, rows, :].astype(F32)
                    elif part_of == i:
                        value = value + rs_in[flow, 0, i, pl.ds(0, 32), :].astype(F32)
                    rs_out[flow, hop, i, rows, :] = value.astype(BF16)
            rs.setdefault((flow, hop), []).append(
                send(
                    rs_out.at[flow, hop, i, pl.ds(0, count)],
                    rs_in.at[flow, hop, i, pl.ds(0, count)],
                    ry_send.at[flow, hop, i], ry_recv.at[flow, hop, i], at_y(step),
                )
            )

    def total(flow):
        source, cols = flow // 2, pl.ds(flow % 2 * WIDE, WIDE)
        for copy in rs[flow, HOPS - 1]:
            copy.wait_recv()
        value = sums[source, pl.ds(0, ROWS), cols]
        for i in range(2):
            value = value + rs_in[flow, HOPS - 1, i].astype(F32)
        return value

    rz = []

    def home(i):
        z_out[i] = total(2 + i).astype(BF16)
        rz.append(send(z_out.at[i], z_in.at[i], rz_send.at[i], rz_recv.at[i], at_z(2)))

    bx = []

    def answer(i):
        value = total(i)
        rz[i].wait_recv()
        value = value + z_in[i].astype(F32)
        reply[i] = (affinity[:, :1] * value).astype(BF16)
        for step in (1, 2, 3):
            bx.append(
                send(
                    reply.at[i, sixteen((t + step) % NX)], returned.at[i, sixteen(t)],
                    bx_send.at[i, step - 1], bx_recv.at[i, step - 1], at_x(step),
                )
            )
        returned[i, sixteen(t), :] = reply[i, sixteen(t), :]

    last = []

    def finish(i):
        for copy in bx[3 * i : 3 * i + 3]:
            copy.wait_recv()
        cols = pl.ds(i * WIDE, WIDE)
        placed = jnp.dot(onehot[...], returned[i], preferred_element_type=F32)
        layer[i] = (hidden[:, cols].astype(F32) + placed.astype(BF16).astype(F32)).astype(BF16)
        last.append(
            send(layer.at[i], out.at[:, cols], hp_send.at[i], hp_recv.at[i], ((p + 1) % NP, e, t))
        )

    back(0, 0)
    back(1, 0)
    down(0, 0)
    back(0, 1)
    back(1, 1)
    for flow in (2, 3):
        for copy in flying[flow]:
            copy.wait_recv()
    up(1, 4)
    down(1, 4)
    back(2, 0)
    back(3, 0)
    down(1, 0)
    for flow, hop in ((2, 1), (3, 1), (2, 2), (3, 2), (2, 3), (3, 3), (0, 2), (1, 2)):
        back(flow, hop)
    home(0)
    back(0, 3)
    home(1)
    back(1, 3)
    answer(0)
    finish(0)
    answer(1)
    finish(1)
    for copy in last:
        copy.wait_recv()
    for copy in pending:
        copy.wait_send()


def shards(context, attn_weight, residual, norm_gain, centroid, w_in, w_out, route_order):
    hbm = pl.BlockSpec(memory_space=pl.ANY)
    dma = pltpu.SemaphoreType.DMA
    flows = (4, HOPS, 2)
    result = pl.pallas_call(
        body,
        out_shape=jax.ShapeDtypeStruct((ROWS, D), BF16),
        in_specs=[hbm] * 8,
        out_specs=hbm,
        scratch_shapes=[
            pltpu.VMEM((4 * ROWS, HEADS), BF16),
            pltpu.VMEM((ROWS, D), BF16),
            pltpu.VMEM((1, D), F32),
            pltpu.VMEM((1, D), BF16),
            pltpu.VMEM((1, ROWS), jnp.int32),
            pltpu.VMEM((NY, 4 * ROWS, HEADS), BF16),
            pltpu.VMEM((NY, 4 * ROWS, 256), BF16),
            pltpu.VMEM((3, NY, ROWS, 256), BF16),
            pltpu.VMEM((ROWS, D), BF16),
            pltpu.VMEM((ROWS, D), BF16),
            pltpu.VMEM((2, NY, ROWS, D), BF16),
            pltpu.VMEM((D, 2 * UNITS), BF16),
            pltpu.VMEM((2 * UNITS, D), BF16),
            pltpu.VMEM((2, NY * ROWS, 2 * UNITS), BF16),
            pltpu.VMEM((2, NY * ROWS, D), F32),
            pltpu.VMEM((4, HOPS, 2, ROWS, WIDE), BF16),
            pltpu.VMEM((4, HOPS, 2, ROWS, WIDE), BF16),
            pltpu.VMEM((2, ROWS, WIDE), BF16),
            pltpu.VMEM((2, ROWS, WIDE), BF16),
            pltpu.VMEM((2, ROWS, WIDE), BF16),
            pltpu.VMEM((2, ROWS, WIDE), BF16),
            pltpu.VMEM((2, ROWS, WIDE), BF16),
            pltpu.VMEM((ROWS, 128), F32),
            pltpu.VMEM((ROWS, ROWS), BF16),
            dma((8,)),
            dma((4,)), dma((4,)),
            dma((3,)), dma((3,)),
            dma(flows), dma(flows),
            dma((4, 3)), dma((4, 3)),
            dma((3,)), dma((3,)),
            dma((2,)), dma((2,)),
            dma(flows), dma(flows),
            dma(flows), dma(flows),
            dma((2,)), dma((2,)),
            dma((2, 3)), dma((2, 3)),
            dma((2,)), dma((2,)),
        ],
        compiler_params=pltpu.CompilerParams(
            collective_id=0, has_side_effects=True, vmem_limit_bytes=60 * 2**20
        ),
        cost_estimate=pl.CostEstimate(
            flops=4_800_000_000, bytes_accessed=4_000_000, transcendentals=600_000
        ),
    )(
        context[0], attn_weight[0].T, residual[0], norm_gain, centroid[0],
        w_in[0, 0], w_out[0, 0], route_order[0],
    )
    return result[None]


def solution(mesh):
    return jax.shard_map(
        shards,
        mesh=mesh,
        in_specs=(
            P("pipe", "expert", "tensor"),
            P("pipe", "tensor", "expert"),
            P("pipe", ("expert", "tensor"), None),
            P("pipe", None),
            P("pipe", "tensor", None),
            P("pipe", "tensor", None, "expert"),
            P("pipe", "tensor", "expert", None),
            P("pipe", ("expert", "tensor"), None),
        ),
        out_specs=P("pipe", ("expert", "tensor"), None),
        check_vma=False,
    )
```

```python
import math

import jax
import jax.numpy as jnp
from jax import lax
from jax.experimental import pallas as pl
from jax.experimental.pallas import tpu as pltpu
from jax.sharding import PartitionSpec as P

MESH = pl.DeviceIdType.MESH
F32, BF16 = jnp.float32, jnp.bfloat16
NY, NZ, NX, NP = 8, 4, 4, 4
D, ROWS, HEADS, UNITS = 2048, 64, 512, 256
WIDE = D // 2
OFFSETS = (0, 1, -1, 2, -2, 3, -3, 4)
SLOT = {0: 0, 1: 1, -1: 2, 2: 3, -2: 4, 3: 5, -3: 6, 4: 7, -4: 7}
HOPS = 4
DIRS = ((0, 1), (1, -1))
GROUPS = ((0, 5), (5, 3))
X_BATCHES = ((0, 3), (3, 2), (5, 2), (7, 1))


def gelu(u):
    inner = math.sqrt(2.0 / math.pi) * (u + 0.044715 * (u * u * u))
    return 0.5 * u * (1.0 + jnp.tanh(inner))


def body(
    ctx_hbm, attn_hbm, res_hbm, gain_hbm, cent_hbm, w_in, w_out, order_hbm, out,
    ctx, res, gain, cent, order, proj, part, from_x, hidden, outgoing, raw, tokens, w1, w2, act, sums,
    rs_out, rs_in, z_out, z_in, reply, returned, layer, affinity, onehot,
    local_sem, wz_send, wz_recv, pz_send, pz_recv, py_send, py_recv, ax_send, ax_recv,
    dx_send, dx_recv, tz_send, tz_recv, ty_send, ty_recv, ry_send, ry_recv,
    rz_send, rz_recv, bx_send, bx_recv, hp_send, hp_recv,
):
    p, e, t = lax.axis_index("pipe"), lax.axis_index("expert"), lax.axis_index("tensor")
    y, z = e // NZ, e % NZ

    def at_y(step):
        return (p, (y + step + NY) % NY * NZ + z, t)

    def at_z(step):
        return (p, y * NZ + (z + step + NZ) % NZ, t)

    def at_x(step):
        return (p, e, (t + step) % NX)

    pending = []

    def send(src, dst, s_sem, r_sem, to):
        copy = pltpu.make_async_remote_copy(
            src_ref=src, dst_ref=dst, send_sem=s_sem, recv_sem=r_sem,
            device_id=to, device_id_type=MESH,
        )
        copy.start()
        pending.append(copy)
        return copy

    barrier = pltpu.get_barrier_semaphore()
    friends = [at_y(1), at_y(-1), at_z(1), at_z(-1), at_z(2), at_x(1), at_x(2), at_x(3)]
    friends += [((p + 1) % NP, e, t), ((p + NP - 1) % NP, e, t)]
    for friend in friends:
        pl.semaphore_signal(barrier, inc=1, device_id=friend, device_id_type=MESH)

    def proj_rows(slot, plane, start=0, count=ROWS):
        return proj.at[slot, pl.ds(pl.multiple_of(plane * ROWS + start, 32), count)]

    loads = [
        pltpu.make_async_copy(src, dst, local_sem.at[i])
        for i, (src, dst) in enumerate((
            (attn_hbm, proj_rows(0, z)), (ctx_hbm, ctx), (res_hbm, res), (gain_hbm, gain),
            (cent_hbm, cent), (order_hbm, order),
            (w_in, w1.at[:, pl.ds(0, UNITS)]), (w_out, w2.at[pl.ds(0, UNITS)]),
        ))
    ]
    for copy in loads:
        copy.start()
    loads[0].wait()
    pl.semaphore_wait(barrier, len(friends))

    planes = (z, (z + NZ - 1) % NZ, (z + 1) % NZ, (z + 2) % NZ)
    pz = [
        send(proj_rows(0, z), proj_rows(0, z), pz_send.at[i], pz_recv.at[i], at_z(step))
        for i, step in enumerate((1, -1, 2))
    ]

    def ring(view, flow, hop, s_sem, r_sem):
        made = []
        for i, step in DIRS:
            part_of = None if hop < HOPS - 1 else i
            src = view(flow, SLOT[-step * hop], part_of)
            dst = view(flow, SLOT[-step * (hop + 1)], part_of)
            made.append(
                send(src, dst, s_sem.at[flow, hop, i], r_sem.at[flow, hop, i], at_y(step))
            )
        return made

    def proj_view(flow, slot, half):
        if half is None:
            return proj_rows(slot, planes[flow])
        return proj_rows(slot, planes[flow], half * 32, 32)

    flying = [ring(proj_view, 0, 0, py_send, py_recv)]

    def pass_columns(flow, hop):
        for copy in flying[flow]:
            copy.wait_recv()
        flying[flow] = ring(proj_view, flow, hop, py_send, py_recv)

    pass_columns(0, 1)

    for flow in (1, 2, 3):
        pz[flow - 1].wait_recv()
        flying.append(ring(proj_view, flow, 0, py_send, py_recv))
        if flow == 2:
            pass_columns(0, 2)

    half = UNITS // 2

    def units(i, start=0, count=half):
        return pl.ds(i * half + start, count), pl.ds(UNITS + i * half + start, count)

    wz_in = []
    for i, step in DIRS:
        mine, there = units(i)
        wz_in.append(
            send(w_in.at[:, mine], w1.at[:, there], wz_send.at[i], wz_recv.at[i], at_z(step))
        )

    wz_out = []

    def send_w_out(piece, start, count):
        for i, step in DIRS:
            mine, there = units(i, start, count)
            k = 2 + 2 * piece + i
            wz_out.append(
                send(w_out.at[mine], w2.at[there], wz_send.at[k], wz_recv.at[k], at_z(step))
            )

    def project(slot):
        value = lax.dot_general(
            ctx[...], proj[slot], (((1,), (1,)), ((), ())), preferred_element_type=F32
        )
        part[slot] = value.astype(BF16)

    def share(batch):
        first, count = X_BATCHES[batch]
        made = []
        for step in (1, 2, 3):
            rows = pl.ds(pl.multiple_of((t + step) % NX * ROWS, ROWS), ROWS)
            made.append(
                send(
                    part.at[pl.ds(first, count), rows],
                    from_x.at[step - 1, pl.ds(first, count)],
                    ax_send.at[batch, step - 1], ax_recv.at[batch, step - 1], at_x(step),
                )
            )
        return made

    loads[1].wait()
    project(0)
    for copy in loads[2:6]:
        copy.wait()
    onehot[...] = (lax.broadcasted_iota(jnp.int32, (ROWS, ROWS), 0) == order[...]).astype(BF16)
    shared = []
    for hop in range(1, HOPS):
        for flow in (1, 2, 3):
            pass_columns(flow, hop)
            if (flow, hop) == (2, 1):
                pass_columns(0, 3)
        project(2 * hop - 1)
        project(2 * hop)
        shared.append(share(hop - 1))

    def sixteen(k):
        return pl.ds(pl.multiple_of(k * 16, 16), 16)

    def block_columns(offset):
        return pl.ds(pl.multiple_of((y + offset + 2 * NY) % NY * 256, 256), 256)

    dx = []

    def dispatch(group, batches):
        first, count = GROUPS[group]
        for batch in batches:
            for copy in shared[batch]:
                copy.wait_recv()
        for slot in range(first, first + count):
            attended = part[
                slot, pl.ds(pl.multiple_of(t * ROWS, ROWS), ROWS), :
            ].astype(F32)
            for other in range(3):
                attended = attended + from_x[other, slot].astype(F32)
            cols = block_columns(OFFSETS[slot])
            value = (res[:, cols].astype(F32) + attended).astype(BF16)
            hidden[:, cols] = value
            picked = lax.dot_general(
                onehot[...], value, (((0,), (0,)), ((), ())), preferred_element_type=F32
            )
            outgoing[slot] = picked.astype(BF16)
        slots = pl.ds(first, count)
        for step in (1, 2, 3):
            dx.append(
                send(
                    outgoing.at[slots, sixteen((t + step) % NX)], raw.at[0, 0, slots, sixteen(t)],
                    dx_send.at[group, step - 1], dx_recv.at[group, step - 1], at_x(step),
                )
            )
        for slot in range(first, first + count):
            raw[0, 0, slot, sixteen(t), :] = outgoing[slot, sixteen(t), :]

    def token_view(flow, slot, half):
        slots = pl.ds(*GROUPS[flow % 2])
        if half is None:
            return raw.at[flow // 2, slot, slots]
        return raw.at[flow // 2, slot, slots, pl.ds(half * 32, 32)]

    tz = []

    def depart(group):
        for copy in dx[3 * group : 3 * group + 3]:
            copy.wait_recv()
        flying_tokens.append(ring(token_view, group, 0, ty_send, ty_recv))
        tz.append(
            send(
                token_view(group, 0, None), token_view(2 + group, 0, None),
                tz_send.at[group], tz_recv.at[group], at_z(2),
            )
        )

    flying_tokens = []
    dispatch(0, (0, 1))
    for flow in range(4):
        for copy in flying[flow]:
            copy.wait_recv()
    project(7)
    shared.append(share(3))
    depart(0)
    dispatch(1, (2, 3))
    depart(1)
    flying = flying_tokens

    def norm(source, slots):
        for slot in slots:
            squares = jnp.zeros((ROWS, 1), F32)
            for q in range(NY):
                value = raw[source, slot, q].astype(F32)
                squares = squares + jnp.sum(value * value, axis=-1, keepdims=True)
            inverse_rms = lax.rsqrt(squares * (1.0 / D) + 1e-05)
            for q in range(NY):
                cols = block_columns(OFFSETS[slot] + OFFSETS[q])
                value = raw[source, slot, q].astype(F32) * inverse_rms * gain[:, cols]
                tokens[source, slot, :, cols] = value.astype(BF16)

    norm(0, (0,))
    dots = jnp.zeros((ROWS, 1), F32)
    for c in range(4):
        cols = pl.ds(c * 512, 512)
        dots = dots + jnp.sum(
            tokens[0, 0, :, cols].astype(F32) * cent[:, cols].astype(F32), axis=-1, keepdims=True
        )
    affinity[...] = jnp.broadcast_to(1.0 / (1.0 + jnp.exp(-dots)), (ROWS, 128))

    def pass_on(flow, hop):
        for copy in flying[flow]:
            copy.wait_recv()
        flying[flow] = ring(token_view, flow, hop, ty_send, ty_recv)

    def up(source, first):
        def tile(j, carry):
            cols = pl.ds(pl.multiple_of(j * 256, 256), 256)
            value = jnp.dot(
                tokens[source, pl.ds(first, 4)].reshape(4 * ROWS, D), w1[:, cols],
                preferred_element_type=F32,
            )
            act[source, pl.ds(first * ROWS, 4 * ROWS), cols] = gelu(value).astype(BF16)
            return carry

        lax.fori_loop(0, 2, tile, 0)

    def down(source, first):
        rows = pl.ds(first * ROWS, 4 * ROWS)

        def tile(j, carry):
            cols = pl.ds(pl.multiple_of(j * 512, 512), 512)
            sums[source, rows, cols] = jnp.dot(
                act[source, rows, :], w2[:, cols], preferred_element_type=F32
            )
            return carry

        lax.fori_loop(0, 4, tile, 0)

    for hop in (1, 2):
        for flow in (0, 1):
            pass_on(flow, hop)
    tz[0].wait_recv()
    flying.append(ring(token_view, 2, 0, ty_send, ty_recv))
    for flow in (0, 1):
        pass_on(flow, 3)
    tz[1].wait_recv()
    flying.append(ring(token_view, 3, 0, ty_send, ty_recv))
    send_w_out(0, 0, half)
    for copy in loads[6:]:
        copy.wait()
    for copy in wz_in:
        copy.wait_recv()
    norm(0, (1, 2, 3))
    up(0, 0)
    for flow in (2, 3):
        pass_on(flow, 1)
    for flow in (0, 1):
        for copy in flying[flow]:
            copy.wait_recv()
    norm(0, (4, 5, 6, 7))
    up(0, 4)
    for flow in (2, 3):
        pass_on(flow, 2)
    norm(1, (0, 1, 2, 3))
    up(1, 0)
    for flow in (2, 3):
        pass_on(flow, 3)
    for copy in wz_out:
        copy.wait_recv()
    down(0, 4)

    rs = {}

    def back(flow, hop):
        source, cols = flow // 2, pl.ds(flow % 2 * WIDE, WIDE)
        for i, step in DIRS:
            start = SLOT[step * (HOPS - hop)] * ROWS
            count = 32 if hop == 0 else ROWS
            if hop == 0:
                rs_out[flow, hop, i, pl.ds(0, 32), :] = sums[
                    source, pl.ds(start + i * 32, 32), cols
                ].astype(BF16)
            else:
                rs[flow, hop - 1][i].wait_recv()
                for part_of in range(2):
                    rows = pl.ds(part_of * 32, 32)
                    value = sums[source, pl.ds(start + part_of * 32, 32), cols]
                    if hop > 1:
                        value = value + rs_in[flow, hop - 1, i, rows, :].astype(F32)
                    elif part_of == i:
                        value = value + rs_in[flow, 0, i, pl.ds(0, 32), :].astype(F32)
                    rs_out[flow, hop, i, rows, :] = value.astype(BF16)
            rs.setdefault((flow, hop), []).append(
                send(
                    rs_out.at[flow, hop, i, pl.ds(0, count)],
                    rs_in.at[flow, hop, i, pl.ds(0, count)],
                    ry_send.at[flow, hop, i], ry_recv.at[flow, hop, i], at_y(step),
                )
            )

    def total(flow):
        source, cols = flow // 2, pl.ds(flow % 2 * WIDE, WIDE)
        for copy in rs[flow, HOPS - 1]:
            copy.wait_recv()
        value = sums[source, pl.ds(0, ROWS), cols]
        for i in range(2):
            value = value + rs_in[flow, HOPS - 1, i].astype(F32)
        return value

    rz = []

    def home(i):
        z_out[i] = total(2 + i).astype(BF16)
        rz.append(send(z_out.at[i], z_in.at[i], rz_send.at[i], rz_recv.at[i], at_z(2)))

    bx = []

    def answer(i):
        value = total(i)
        rz[i].wait_recv()
        value = value + z_in[i].astype(F32)
        reply[i] = (affinity[:, :1] * value).astype(BF16)
        for step in (1, 2, 3):
            bx.append(
                send(
                    reply.at[i, sixteen((t + step) % NX)], returned.at[i, sixteen(t)],
                    bx_send.at[i, step - 1], bx_recv.at[i, step - 1], at_x(step),
                )
            )
        returned[i, sixteen(t), :] = reply[i, sixteen(t), :]

    last = []

    def finish(i):
        for copy in bx[3 * i : 3 * i + 3]:
            copy.wait_recv()
        cols = pl.ds(i * WIDE, WIDE)
        placed = jnp.dot(onehot[...], returned[i], preferred_element_type=F32)
        layer[i] = (hidden[:, cols].astype(F32) + placed.astype(BF16).astype(F32)).astype(BF16)
        last.append(
            send(layer.at[i], out.at[:, cols], hp_send.at[i], hp_recv.at[i], ((p + 1) % NP, e, t))
        )

    back(0, 0)
    back(1, 0)
    down(0, 0)
    back(0, 1)
    back(1, 1)
    for flow in (2, 3):
        for copy in flying[flow]:
            copy.wait_recv()
    norm(1, (4, 5, 6, 7))
    up(1, 4)
    down(1, 4)
    back(2, 0)
    back(3, 0)
    down(1, 0)
    for flow, hop in ((2, 1), (3, 1), (2, 2), (3, 2), (2, 3), (0, 2), (3, 3), (1, 2)):
        back(flow, hop)
    home(0)
    back(0, 3)
    home(1)
    back(1, 3)
    answer(0)
    answer(1)
    finish(0)
    finish(1)
    for copy in last:
        copy.wait_recv()
    for copy in pending:
        copy.wait_send()


def shards(context, attn_weight, residual, norm_gain, centroid, w_in, w_out, route_order):
    hbm = pl.BlockSpec(memory_space=pl.ANY)
    dma = pltpu.SemaphoreType.DMA
    flows = (4, HOPS, 2)
    result = pl.pallas_call(
        body,
        out_shape=jax.ShapeDtypeStruct((ROWS, D), BF16),
        in_specs=[hbm] * 8,
        out_specs=hbm,
        scratch_shapes=[
            pltpu.VMEM((4 * ROWS, HEADS), BF16),
            pltpu.VMEM((ROWS, D), BF16),
            pltpu.VMEM((1, D), F32),
            pltpu.VMEM((1, D), BF16),
            pltpu.VMEM((1, ROWS), jnp.int32),
            pltpu.VMEM((NY, 4 * ROWS, HEADS), BF16),
            pltpu.VMEM((NY, 4 * ROWS, 256), BF16),
            pltpu.VMEM((3, NY, ROWS, 256), BF16),
            pltpu.VMEM((ROWS, D), BF16),
            pltpu.VMEM((NY, ROWS, 256), BF16),
            pltpu.VMEM((2, NY, NY, ROWS, 256), BF16),
            pltpu.VMEM((2, NY, ROWS, D), BF16),
            pltpu.VMEM((D, 2 * UNITS), BF16),
            pltpu.VMEM((2 * UNITS, D), BF16),
            pltpu.VMEM((2, NY * ROWS, 2 * UNITS), BF16),
            pltpu.VMEM((2, NY * ROWS, D), F32),
            pltpu.VMEM((4, HOPS, 2, ROWS, WIDE), BF16),
            pltpu.VMEM((4, HOPS, 2, ROWS, WIDE), BF16),
            pltpu.VMEM((2, ROWS, WIDE), BF16),
            pltpu.VMEM((2, ROWS, WIDE), BF16),
            pltpu.VMEM((2, ROWS, WIDE), BF16),
            pltpu.VMEM((2, ROWS, WIDE), BF16),
            pltpu.VMEM((2, ROWS, WIDE), BF16),
            pltpu.VMEM((ROWS, 128), F32),
            pltpu.VMEM((ROWS, ROWS), BF16),
            dma((8,)),
            dma((4,)), dma((4,)),
            dma((3,)), dma((3,)),
            dma(flows), dma(flows),
            dma((4, 3)), dma((4, 3)),
            dma((2, 3)), dma((2, 3)),
            dma((2,)), dma((2,)),
            dma(flows), dma(flows),
            dma(flows), dma(flows),
            dma((2,)), dma((2,)),
            dma((2, 3)), dma((2, 3)),
            dma((2,)), dma((2,)),
        ],
        compiler_params=pltpu.CompilerParams(
            collective_id=0, has_side_effects=True, vmem_limit_bytes=60 * 2**20
        ),
        cost_estimate=pl.CostEstimate(
            flops=4_800_000_000, bytes_accessed=4_000_000, transcendentals=600_000
        ),
    )(
        context[0], attn_weight[0].T, residual[0], norm_gain, centroid[0],
        w_in[0, 0], w_out[0, 0], route_order[0],
    )
    return result[None]


def solution(mesh):
    return jax.shard_map(
        shards,
        mesh=mesh,
        in_specs=(
            P("pipe", "expert", "tensor"),
            P("pipe", "tensor", "expert"),
            P("pipe", ("expert", "tensor"), None),
            P("pipe", None),
            P("pipe", "tensor", None),
            P("pipe", "tensor", None, "expert"),
            P("pipe", "tensor", "expert", None),
            P("pipe", ("expert", "tensor"), None),
        ),
        out_specs=P("pipe", ("expert", "tensor"), None),
        check_vma=False,
    )
```

```python
import math

import jax
import jax.numpy as jnp
from jax import lax
from jax.experimental import pallas as pl
from jax.experimental.pallas import tpu as pltpu
from jax.sharding import PartitionSpec as P

MESH = pl.DeviceIdType.MESH
F32, BF16 = jnp.float32, jnp.bfloat16
NY, NZ, NX, NP = 8, 4, 4, 4
D, ROWS, HEADS, UNITS = 2048, 64, 512, 256
WIDE = D // 2
OFFSETS = (0, 1, -1, 2, -2, 3, -3, 4)
SLOT = {0: 0, 1: 1, -1: 2, 2: 3, -2: 4, 3: 5, -3: 6, 4: 7, -4: 7}
HOPS = 4
DIRS = ((0, 1), (1, -1))
GROUPS = ((0, 5), (5, 3))
X_BATCHES = ((0, 3), (3, 2), (5, 2), (7, 1))


def gelu(u):
    inner = math.sqrt(2.0 / math.pi) * (u + 0.044715 * (u * u * u))
    return 0.5 * u * (1.0 + jnp.tanh(inner))


def body(
    ctx_hbm, attn_hbm, res_hbm, gain_hbm, cent_hbm, w_in, w_out, order_hbm, out,
    ctx, res, gain, cent, order, proj, part, from_x, hidden, outgoing, raw, tokens, w1, w2, act, sums,
    rs_out, rs_in, z_out, z_in, reply, returned, layer, affinity, onehot,
    local_sem, wz_send, wz_recv, pz_send, pz_recv, py_send, py_recv, ax_send, ax_recv,
    dx_send, dx_recv, tz_send, tz_recv, ty_send, ty_recv, ry_send, ry_recv,
    rz_send, rz_recv, bx_send, bx_recv, hp_send, hp_recv,
):
    p, e, t = lax.axis_index("pipe"), lax.axis_index("expert"), lax.axis_index("tensor")
    y, z = e // NZ, e % NZ

    def at_y(step):
        return (p, (y + step + NY) % NY * NZ + z, t)

    def at_z(step):
        return (p, y * NZ + (z + step + NZ) % NZ, t)

    def at_x(step):
        return (p, e, (t + step) % NX)

    pending = []

    def send(src, dst, s_sem, r_sem, to):
        copy = pltpu.make_async_remote_copy(
            src_ref=src, dst_ref=dst, send_sem=s_sem, recv_sem=r_sem,
            device_id=to, device_id_type=MESH,
        )
        copy.start()
        pending.append(copy)
        return copy

    barrier = pltpu.get_barrier_semaphore()
    friends = [at_y(1), at_y(-1), at_z(1), at_z(-1), at_z(2), at_x(1), at_x(2), at_x(3)]
    friends += [((p + 1) % NP, e, t), ((p + NP - 1) % NP, e, t)]
    for friend in friends:
        pl.semaphore_signal(barrier, inc=1, device_id=friend, device_id_type=MESH)

    def proj_rows(slot, plane, start=0, count=ROWS):
        return proj.at[slot, pl.ds(pl.multiple_of(plane * ROWS + start, 32), count)]

    loads = [
        pltpu.make_async_copy(src, dst, local_sem.at[i])
        for i, (src, dst) in enumerate((
            (attn_hbm, proj_rows(0, z)), (ctx_hbm, ctx), (res_hbm, res), (gain_hbm, gain),
            (cent_hbm, cent), (order_hbm, order),
            (w_in, w1.at[:, pl.ds(0, UNITS)]), (w_out, w2.at[pl.ds(0, UNITS)]),
        ))
    ]
    for copy in loads:
        copy.start()
    loads[0].wait()
    pl.semaphore_wait(barrier, len(friends))

    planes = (z, (z + NZ - 1) % NZ, (z + 1) % NZ, (z + 2) % NZ)
    pz = [
        send(proj_rows(0, z), proj_rows(0, z), pz_send.at[i], pz_recv.at[i], at_z(step))
        for i, step in enumerate((1, -1, 2))
    ]

    def ring(view, flow, hop, s_sem, r_sem):
        made = []
        for i, step in DIRS:
            part_of = None if hop < HOPS - 1 else i
            src = view(flow, SLOT[-step * hop], part_of)
            dst = view(flow, SLOT[-step * (hop + 1)], part_of)
            made.append(
                send(src, dst, s_sem.at[flow, hop, i], r_sem.at[flow, hop, i], at_y(step))
            )
        return made

    def proj_view(flow, slot, half):
        if half is None:
            return proj_rows(slot, planes[flow])
        return proj_rows(slot, planes[flow], half * 32, 32)

    flying = [ring(proj_view, 0, 0, py_send, py_recv)]

    def pass_columns(flow, hop):
        for copy in flying[flow]:
            copy.wait_recv()
        flying[flow] = ring(proj_view, flow, hop, py_send, py_recv)

    pass_columns(0, 1)

    for flow in (1, 2, 3):
        pz[flow - 1].wait_recv()
        flying.append(ring(proj_view, flow, 0, py_send, py_recv))
        if flow == 2:
            pass_columns(0, 2)

    half = UNITS // 2

    def units(i, start=0, count=half):
        return pl.ds(i * half + start, count), pl.ds(UNITS + i * half + start, count)

    wz_in = []
    for i, step in DIRS:
        mine, there = units(i)
        wz_in.append(
            send(w_in.at[:, mine], w1.at[:, there], wz_send.at[i], wz_recv.at[i], at_z(step))
        )

    wz_out = []

    def send_w_out(piece, start, count):
        for i, step in DIRS:
            mine, there = units(i, start, count)
            k = 2 + 2 * piece + i
            wz_out.append(
                send(w_out.at[mine], w2.at[there], wz_send.at[k], wz_recv.at[k], at_z(step))
            )

    def project(slot):
        value = lax.dot_general(
            ctx[...], proj[slot], (((1,), (1,)), ((), ())), preferred_element_type=F32
        )
        part[slot] = value.astype(BF16)

    def share(batch):
        first, count = X_BATCHES[batch]
        made = []
        for step in (1, 2, 3):
            rows = pl.ds(pl.multiple_of((t + step) % NX * ROWS, ROWS), ROWS)
            made.append(
                send(
                    part.at[pl.ds(first, count), rows],
                    from_x.at[step - 1, pl.ds(first, count)],
                    ax_send.at[batch, step - 1], ax_recv.at[batch, step - 1], at_x(step),
                )
            )
        return made

    loads[1].wait()
    project(0)
    for copy in loads[2:6]:
        copy.wait()
    onehot[...] = (lax.broadcasted_iota(jnp.int32, (ROWS, ROWS), 0) == order[...]).astype(BF16)
    shared = []
    for hop in range(1, HOPS):
        for flow in (1, 2, 3):
            pass_columns(flow, hop)
            if (flow, hop) == (2, 1):
                pass_columns(0, 3)
        project(2 * hop - 1)
        project(2 * hop)
        shared.append(share(hop - 1))

    def sixteen(k):
        return pl.ds(pl.multiple_of(k * 16, 16), 16)

    def block_columns(offset):
        return pl.ds(pl.multiple_of((y + offset + 2 * NY) % NY * 256, 256), 256)

    dx = []

    def dispatch(group, batches):
        first, count = GROUPS[group]
        for batch in batches:
            for copy in shared[batch]:
                copy.wait_recv()
        for slot in range(first, first + count):
            attended = part[
                slot, pl.ds(pl.multiple_of(t * ROWS, ROWS), ROWS), :
            ].astype(F32)
            for other in range(3):
                attended = attended + from_x[other, slot].astype(F32)
            cols = block_columns(OFFSETS[slot])
            value = (res[:, cols].astype(F32) + attended).astype(BF16)
            hidden[:, cols] = value
            picked = lax.dot_general(
                onehot[...], value, (((0,), (0,)), ((), ())), preferred_element_type=F32
            )
            outgoing[slot] = picked.astype(BF16)
        slots = pl.ds(first, count)
        for step in (1, 2, 3):
            dx.append(
                send(
                    outgoing.at[slots, sixteen((t + step) % NX)], raw.at[0, 0, slots, sixteen(t)],
                    dx_send.at[group, step - 1], dx_recv.at[group, step - 1], at_x(step),
                )
            )
        for slot in range(first, first + count):
            raw[0, 0, slot, sixteen(t), :] = outgoing[slot, sixteen(t), :]

    def token_view(flow, slot, half):
        slots = pl.ds(*GROUPS[flow % 2])
        if half is None:
            return raw.at[flow // 2, slot, slots]
        return raw.at[flow // 2, slot, slots, pl.ds(half * 32, 32)]

    tz = []

    def depart(group):
        for copy in dx[3 * group : 3 * group + 3]:
            copy.wait_recv()
        flying_tokens.append(ring(token_view, group, 0, ty_send, ty_recv))
        tz.append(
            send(
                token_view(group, 0, None), token_view(2 + group, 0, None),
                tz_send.at[group], tz_recv.at[group], at_z(2),
            )
        )

    flying_tokens = []
    dispatch(0, (0, 1))
    for flow in range(4):
        for copy in flying[flow]:
            copy.wait_recv()
    project(7)
    shared.append(share(3))
    depart(0)
    dispatch(1, (2, 3))
    depart(1)
    flying = flying_tokens

    def norm(source, slots):
        for slot in slots:
            squares = jnp.zeros((ROWS, 1), F32)
            for q in range(NY):
                value = raw[source, slot, q].astype(F32)
                squares = squares + jnp.sum(value * value, axis=-1, keepdims=True)
            inverse_rms = lax.rsqrt(squares * (1.0 / D) + 1e-05)
            for q in range(NY):
                cols = block_columns(OFFSETS[slot] + OFFSETS[q])
                value = raw[source, slot, q].astype(F32) * inverse_rms * gain[:, cols]
                tokens[source, slot, :, cols] = value.astype(BF16)

    norm(0, (0,))
    dots = jnp.zeros((ROWS, 1), F32)
    for c in range(4):
        cols = pl.ds(c * 512, 512)
        dots = dots + jnp.sum(
            tokens[0, 0, :, cols].astype(F32) * cent[:, cols].astype(F32), axis=-1, keepdims=True
        )
    affinity[...] = jnp.broadcast_to(1.0 / (1.0 + jnp.exp(-dots)), (ROWS, 128))

    def pass_on(flow, hop):
        for copy in flying[flow]:
            copy.wait_recv()
        flying[flow] = ring(token_view, flow, hop, ty_send, ty_recv)

    def up(source, first):
        def tile(j, carry):
            cols = pl.ds(pl.multiple_of(j * 256, 256), 256)
            value = jnp.dot(
                tokens[source, pl.ds(first, 4)].reshape(4 * ROWS, D), w1[:, cols],
                preferred_element_type=F32,
            )
            act[source, pl.ds(first * ROWS, 4 * ROWS), cols] = gelu(value).astype(BF16)
            return carry

        lax.fori_loop(0, 2, tile, 0)

    def down(source, first):
        rows = pl.ds(first * ROWS, 4 * ROWS)

        def tile(j, carry):
            cols = pl.ds(pl.multiple_of(j * 512, 512), 512)
            sums[source, rows, cols] = jnp.dot(
                act[source, rows, :], w2[:, cols], preferred_element_type=F32
            )
            return carry

        lax.fori_loop(0, 4, tile, 0)

    for hop in (1, 2):
        for flow in (0, 1):
            pass_on(flow, hop)
    tz[0].wait_recv()
    flying.append(ring(token_view, 2, 0, ty_send, ty_recv))
    pass_on(0, 3)
    tz[1].wait_recv()
    flying.append(ring(token_view, 3, 0, ty_send, ty_recv))
    send_w_out(0, 0, half)
    pass_on(1, 3)
    for copy in loads[6:]:
        copy.wait()
    for copy in wz_in:
        copy.wait_recv()
    norm(0, (1, 2, 3))
    up(0, 0)
    for flow in (2, 3):
        pass_on(flow, 1)
    for flow in (0, 1):
        for copy in flying[flow]:
            copy.wait_recv()
    norm(0, (4, 5, 6, 7))
    up(0, 4)
    for flow in (2, 3):
        pass_on(flow, 2)
    norm(1, (0, 1, 2, 3))
    up(1, 0)
    for flow in (2, 3):
        pass_on(flow, 3)
    for copy in wz_out:
        copy.wait_recv()
    down(0, 4)

    rs = {}

    def back(flow, hop):
        source, cols = flow // 2, pl.ds(flow % 2 * WIDE, WIDE)
        for i, step in DIRS:
            start = SLOT[step * (HOPS - hop)] * ROWS
            count = 32 if hop == 0 else ROWS
            if hop == 0:
                rs_out[flow, hop, i, pl.ds(0, 32), :] = sums[
                    source, pl.ds(start + i * 32, 32), cols
                ].astype(BF16)
            else:
                rs[flow, hop - 1][i].wait_recv()
                for part_of in range(2):
                    rows = pl.ds(part_of * 32, 32)
                    value = sums[source, pl.ds(start + part_of * 32, 32), cols]
                    if hop > 1:
                        value = value + rs_in[flow, hop - 1, i, rows, :].astype(F32)
                    elif part_of == i:
                        value = value + rs_in[flow, 0, i, pl.ds(0, 32), :].astype(F32)
                    rs_out[flow, hop, i, rows, :] = value.astype(BF16)
            rs.setdefault((flow, hop), []).append(
                send(
                    rs_out.at[flow, hop, i, pl.ds(0, count)],
                    rs_in.at[flow, hop, i, pl.ds(0, count)],
                    ry_send.at[flow, hop, i], ry_recv.at[flow, hop, i], at_y(step),
                )
            )

    def total(flow):
        source, cols = flow // 2, pl.ds(flow % 2 * WIDE, WIDE)
        for copy in rs[flow, HOPS - 1]:
            copy.wait_recv()
        value = sums[source, pl.ds(0, ROWS), cols]
        for i in range(2):
            value = value + rs_in[flow, HOPS - 1, i].astype(F32)
        return value

    rz = []

    def home(i):
        z_out[i] = total(2 + i).astype(BF16)
        rz.append(send(z_out.at[i], z_in.at[i], rz_send.at[i], rz_recv.at[i], at_z(2)))

    bx = []

    def answer(i):
        value = total(i)
        rz[i].wait_recv()
        value = value + z_in[i].astype(F32)
        reply[i] = (affinity[:, :1] * value).astype(BF16)
        for step in (1, 2, 3):
            bx.append(
                send(
                    reply.at[i, sixteen((t + step) % NX)], returned.at[i, sixteen(t)],
                    bx_send.at[i, step - 1], bx_recv.at[i, step - 1], at_x(step),
                )
            )
        returned[i, sixteen(t), :] = reply[i, sixteen(t), :]

    last = []

    def finish(i):
        for copy in bx[3 * i : 3 * i + 3]:
            copy.wait_recv()
        cols = pl.ds(i * WIDE, WIDE)
        placed = jnp.dot(onehot[...], returned[i], preferred_element_type=F32)
        layer[i] = (hidden[:, cols].astype(F32) + placed.astype(BF16).astype(F32)).astype(BF16)
        last.append(
            send(layer.at[i], out.at[:, cols], hp_send.at[i], hp_recv.at[i], ((p + 1) % NP, e, t))
        )

    back(0, 0)
    back(1, 0)
    down(0, 0)
    back(0, 1)
    back(1, 1)
    for flow in (2, 3):
        for copy in flying[flow]:
            copy.wait_recv()
    norm(1, (4, 5, 6, 7))
    up(1, 4)
    down(1, 4)
    back(2, 0)
    back(3, 0)
    down(1, 0)
    for flow, hop in ((2, 1), (3, 1), (2, 2), (3, 2), (2, 3), (0, 2), (3, 3), (1, 2)):
        back(flow, hop)
    home(0)
    back(0, 3)
    home(1)
    back(1, 3)
    answer(0)
    answer(1)
    finish(0)
    finish(1)
    for copy in last:
        copy.wait_recv()
    for copy in pending:
        copy.wait_send()


def shards(context, attn_weight, residual, norm_gain, centroid, w_in, w_out, route_order):
    hbm = pl.BlockSpec(memory_space=pl.ANY)
    dma = pltpu.SemaphoreType.DMA
    flows = (4, HOPS, 2)
    result = pl.pallas_call(
        body,
        out_shape=jax.ShapeDtypeStruct((ROWS, D), BF16),
        in_specs=[hbm] * 8,
        out_specs=hbm,
        scratch_shapes=[
            pltpu.VMEM((4 * ROWS, HEADS), BF16),
            pltpu.VMEM((ROWS, D), BF16),
            pltpu.VMEM((1, D), F32),
            pltpu.VMEM((1, D), BF16),
            pltpu.VMEM((1, ROWS), jnp.int32),
            pltpu.VMEM((NY, 4 * ROWS, HEADS), BF16),
            pltpu.VMEM((NY, 4 * ROWS, 256), BF16),
            pltpu.VMEM((3, NY, ROWS, 256), BF16),
            pltpu.VMEM((ROWS, D), BF16),
            pltpu.VMEM((NY, ROWS, 256), BF16),
            pltpu.VMEM((2, NY, NY, ROWS, 256), BF16),
            pltpu.VMEM((2, NY, ROWS, D), BF16),
            pltpu.VMEM((D, 2 * UNITS), BF16),
            pltpu.VMEM((2 * UNITS, D), BF16),
            pltpu.VMEM((2, NY * ROWS, 2 * UNITS), BF16),
            pltpu.VMEM((2, NY * ROWS, D), F32),
            pltpu.VMEM((4, HOPS, 2, ROWS, WIDE), BF16),
            pltpu.VMEM((4, HOPS, 2, ROWS, WIDE), BF16),
            pltpu.VMEM((2, ROWS, WIDE), BF16),
            pltpu.VMEM((2, ROWS, WIDE), BF16),
            pltpu.VMEM((2, ROWS, WIDE), BF16),
            pltpu.VMEM((2, ROWS, WIDE), BF16),
            pltpu.VMEM((2, ROWS, WIDE), BF16),
            pltpu.VMEM((ROWS, 128), F32),
            pltpu.VMEM((ROWS, ROWS), BF16),
            dma((8,)),
            dma((4,)), dma((4,)),
            dma((3,)), dma((3,)),
            dma(flows), dma(flows),
            dma((4, 3)), dma((4, 3)),
            dma((2, 3)), dma((2, 3)),
            dma((2,)), dma((2,)),
            dma(flows), dma(flows),
            dma(flows), dma(flows),
            dma((2,)), dma((2,)),
            dma((2, 3)), dma((2, 3)),
            dma((2,)), dma((2,)),
        ],
        compiler_params=pltpu.CompilerParams(
            collective_id=0, has_side_effects=True, vmem_limit_bytes=60 * 2**20
        ),
        cost_estimate=pl.CostEstimate(
            flops=4_800_000_000, bytes_accessed=4_000_000, transcendentals=600_000
        ),
    )(
        context[0], attn_weight[0].T, residual[0], norm_gain, centroid[0],
        w_in[0, 0], w_out[0, 0], route_order[0],
    )
    return result[None]


def solution(mesh):
    return jax.shard_map(
        shards,
        mesh=mesh,
        in_specs=(
            P("pipe", "expert", "tensor"),
            P("pipe", "tensor", "expert"),
            P("pipe", ("expert", "tensor"), None),
            P("pipe", None),
            P("pipe", "tensor", None),
            P("pipe", "tensor", None, "expert"),
            P("pipe", "tensor", "expert", None),
            P("pipe", ("expert", "tensor"), None),
        ),
        out_specs=P("pipe", ("expert", "tensor"), None),
        check_vma=False,
    )
```
